32 devices in a mesh: grp: 2 (over y), pb: 4 (over z), ha: 4 (over x, core).
Axes of the slice: x: 2, y: 2, z: 4, core: 2. Of those that a mesh axis runs over, the one named last changes fastest.
Arguments:
- latents: bfloat16 [8, 384, 3072], P(('grp', 'pb'), None, 'ha'), parts along dimension 0, may hold values from -6 to 6
- timesteps: int32 [8], P(('grp', 'pb')), parts along dimension 0, may hold values from 0 to 999
- mod_weight: bfloat16 [256, 3, 3072], P(None, None, 'ha'), may hold values from -0.375 to 0.375
- qkv_weight: bfloat16 [3072, 3, 3072], P(None, None, 'ha'), may hold values from -0.109375 to 0.109375
- out_weight: bfloat16 [3072, 3072], P('ha'), may hold values from -0.15625 to 0.15625
- noise_frame: bfloat16 [768, 3072], P('grp', 'ha'), parts along dimension 0, may hold values from -6 to 6
Outputs:
- advanced: bfloat16 [8, 384, 3072], P(('grp', 'pb'), None, 'ha'), parts along dimension 0
- queue_next: bfloat16 [8, 384, 3072], P(('grp', 'pb'), None, 'ha'), parts along dimension 0
The draws below stay inside these ranges and needn't reach their ends.
There are 2 independent parts, one for each index of `grp`. The reference program is written for one: setup_inputs(seed, part) draws one part's arguments, and reference() takes and returns one part's arrays. A program takes and returns all parts, laid end to end along the dimension named above; an argument that names none is the same for every part. Nothing has to cross between parts.
All inputs are finite; a program needn't handle non-finite values.
Results may differ from the reference program's by a relative error of at most 0.0045.
Values may be sent and summed in bfloat16 or wider, within the bound.
A program may use at most 64 MiB of HBM per device.

```python
import math
import jax
import jax.numpy as jnp
from jax import lax

D = 3072
HEADS = 24
HD = 128
TDIM = 256
TOK_F = 384
FRAMES = 4


def draw_latents(key, part):
    noise_key = jax.random.fold_in(key, 11)
    direction_key = jax.random.fold_in(key, 12)
    sign_key = jax.random.fold_in(key, 13)
    noise_part = jax.random.normal(noise_key, (FRAMES, TOK_F, D), jnp.float32)
    direction = jax.random.normal(direction_key, (FRAMES, 1, D), jnp.float32)
    token_signs = (2 * jax.random.randint(sign_key, (FRAMES, TOK_F, 1), 0, 2) - 1).astype(jnp.float32)
    values = 0.71 * (noise_part + token_signs * direction)
    return jnp.clip(values, -6.0, 6.0).astype(jnp.bfloat16)


def set_ends(entries, rng, smallest, top_value):
    longest = entries.shape.index(max(entries.shape))
    spots = []
    for shift in (0, 1):
        where = [jax.random.randint(jax.random.fold_in(rng, axis), (), 0, length) for axis, length in enumerate(entries.shape)]
        where[longest] = (where[longest] + shift) % entries.shape[longest]
        spots.append(tuple(where))
    return entries.at[spots[0]].set(smallest).at[spots[1]].set(top_value)


def raised(result, stream_key, source, target, shards_of, factor):
    def block_of(dim):
        return (jnp.arange(result.shape[dim]) // (result.shape[dim] // shards_of)).reshape((-1,) + (1,) * (result.ndim - 1 - dim))

    one_side = jax.random.permutation(stream_key, shards_of)[block_of(target)]
    far = (block_of(target) + shards_of // 2) % shards_of
    return jnp.where((block_of(source) == one_side) | (block_of(source) == far), factor * result, result)


def steps_of(key, dims, shards, low, high):
    gain = 1.0
    for position, blocks in shards:
        draws = jax.random.uniform(jax.random.fold_in(jax.random.fold_in(key, 6), position), (blocks,), jnp.float32, low / len(shards), high / len(shards))
        gain = gain * jnp.repeat(jnp.exp(draws), dims[position] // blocks).reshape((-1,) + (1,) * (len(dims) - 1 - position))
    return gain


def gaussian(rng, shape, spread, limit, pieces=(), kind=jnp.bfloat16):
    entries = jax.random.normal(rng, shape, jnp.float32) * spread
    if len(pieces) > 0:
        entries = steps_of(rng, shape, pieces, -0.22, 0.18) * entries
    return jnp.clip(entries, min=-limit, max=limit).astype(kind)


def gaussian_with(own_key, dims, deviation, limit, pieces, heavy, kind=jnp.bfloat16):
    entries = deviation * jax.random.normal(own_key, dims, jnp.float32)
    if pieces:
        entries = entries * steps_of(own_key, dims, pieces, -0.22, 0.18)
    return jnp.clip(raised(entries, jax.random.fold_in(own_key, 3), *heavy), -limit, limit).astype(kind)


def setup_inputs(seed: int = 0, part: int = 0) -> dict:
    key_list = jax.random.split(jax.random.key(seed), 7)
    part_splits = jax.random.split(jax.random.fold_in(key_list[6], part), 7)
    return {
        "latents": draw_latents(jax.random.fold_in(jax.random.fold_in(key_list[6], part), 71), part),
        "timesteps": set_ends(jax.random.randint(part_splits[1], (FRAMES,), 0, 1000), jax.random.fold_in(part_splits[1], 1), 0, 999).astype(jnp.int32),
        "mod_weight": gaussian(key_list[2], (TDIM, 3, D), TDIM ** -0.5, 0.375, ((2, 4),)),
        "qkv_weight": gaussian(key_list[3], (D, 3, D), D ** -0.5, 0.109375, ((2, 4),)),
        "out_weight": gaussian_with(key_list[4], (D, D), D ** -0.5, 0.15625, ((0, 4),), (0, 1, 4, 2.0)),
        "noise_frame": gaussian(part_splits[5], (TOK_F, D), 1.0, 6.0, ((1, 4),)),
    }


def sinusoid(timesteps):
    half_width = TDIM // 2
    frequency = jnp.exp(-math.log(10000.0) * jnp.arange(half_width, dtype=jnp.float32) / half_width)
    angles = timesteps.astype(jnp.float32)[:, None] * frequency[None, :]
    return jnp.concatenate([jnp.cos(angles), jnp.sin(angles)], axis=1)

def unit_rms(vectors):
    return vectors * lax.rsqrt(lax.optimization_barrier(jnp.mean(vectors * vectors, axis=-1, keepdims=True)) + 1e-06)

def reference(latents, timesteps, mod_weight, qkv_weight, out_weight, noise_frame):
    frames = latents.shape[0]
    embedding = sinusoid(timesteps).astype(jnp.bfloat16)
    modulation = jnp.dot(embedding, mod_weight.reshape(TDIM, 3 * D), preferred_element_type=jnp.float32)
    modulation = modulation.astype(jnp.bfloat16).reshape(frames, 3, D).astype(jnp.float32)
    latent_wide = latents.astype(jnp.float32)
    row_mean = lax.optimization_barrier(jnp.mean(latent_wide, axis=-1, keepdims=True))
    centered = latent_wide - row_mean
    row_var = lax.optimization_barrier(jnp.mean(centered * centered, axis=-1, keepdims=True))
    normed = centered * lax.rsqrt(row_var + 1e-06)
    hidden = normed * (1.0 + modulation[:, 1][:, None, :]) + modulation[:, 0][:, None, :]
    hidden = hidden.astype(jnp.bfloat16).reshape(frames * TOK_F, D)
    projected = jnp.dot(hidden, qkv_weight.reshape(D, 3 * D), preferred_element_type=jnp.float32)
    projected = projected.reshape(frames * TOK_F, 3, HEADS, HD)
    queries = (unit_rms(projected[:, 0]) / math.sqrt(HD)).astype(jnp.bfloat16)
    key_rows = unit_rms(projected[:, 1]).astype(jnp.bfloat16).astype(jnp.float32)
    value_rows = projected[:, 2].astype(jnp.bfloat16).astype(jnp.float32)

    def attend_frame(query_frame):
        scores = jnp.einsum('qhd,khd->hqk', query_frame.astype(jnp.float32), key_rows)
        weights_exp = jnp.exp(scores)
        denominator = lax.optimization_barrier(jnp.sum(weights_exp, axis=2))
        numerator = jnp.einsum('hqk,khd->qhd', weights_exp.astype(jnp.bfloat16).astype(jnp.float32), value_rows)
        return (numerator / denominator.T[:, :, None]).astype(jnp.bfloat16)
    attended = lax.map(attend_frame, queries.reshape(frames, TOK_F, HEADS, HD))
    attended = attended.reshape(frames * TOK_F, D)
    branch = jnp.dot(attended, out_weight, preferred_element_type=jnp.float32).reshape(frames, TOK_F, D)
    advanced = (latent_wide + modulation[:, 2][:, None, :] * branch).astype(jnp.bfloat16)
    queue_next = jnp.concatenate([advanced[1:], noise_frame[None]], axis=0)
    return (advanced, queue_next)
```

```python
import functools
import math

import jax
import jax.numpy as jnp
from jax import lax
from jax.experimental import pallas as pl
from jax.experimental.pallas import tpu as pltpu
from jax.sharding import PartitionSpec as P

HD = 128
TDIM = 256


def from_behind(x, axis, by):
    size = lax.axis_size(axis)
    pairs = [(i, i + by) for i in range(size) if 0 <= i + by < size]
    return lax.ppermute(x, axis, pairs)


def sinusoid(timesteps):
    half_width = TDIM // 2
    frequency = jnp.exp(-math.log(10000.0) * jnp.arange(half_width, dtype=jnp.float32) / half_width)
    angles = timesteps.astype(jnp.float32)[:, None] * frequency[None, :]
    return jnp.concatenate([jnp.cos(angles), jnp.sin(angles)], axis=1)


def unit_rms(vectors):
    return vectors * lax.rsqrt(jnp.mean(vectors * vectors, axis=-1, keepdims=True) + 1e-06)


def absorb(running, pieces, queries, head_local):
    key_piece, value_piece = pieces

    def one_frame(position, inner):
        numerator, denominator = inner
        key_frame = lax.dynamic_index_in_dim(key_piece, position, 0, keepdims=False)
        value_frame = lax.dynamic_index_in_dim(value_piece, position, 0, keepdims=False)
        key_count = key_frame.shape[0]
        key_frame = key_frame.reshape(key_count, head_local, -1)
        value_frame = value_frame.reshape(key_count, head_local, -1)
        scores = jnp.einsum("rhd,khd->hrk", queries, key_frame, preferred_element_type=jnp.float32)
        weights_exp = jnp.exp(scores)
        denominator = denominator + jnp.sum(weights_exp, axis=2)
        numerator = numerator + jnp.einsum(
            "hrk,khd->rhd",
            weights_exp.astype(jnp.bfloat16),
            value_frame,
            preferred_element_type=jnp.float32,
        )
        return (numerator, denominator)

    return lax.fori_loop(0, key_piece.shape[0], one_frame, running)


def on_device(latents, timesteps, mod_weight, qkv_weight, out_weight, noise_frame):
    frames, tok_count, local_width = latents.shape
    full_width = qkv_weight.shape[0]
    head_size = HD
    head_local = local_width // head_size
    row_count = frames * tok_count
    out_columns = lax.all_to_all(out_weight, "ha", split_axis=1, concat_axis=0, tiled=True)
    embedding = sinusoid(timesteps).astype(jnp.bfloat16)
    modulation = jnp.dot(
        embedding,
        mod_weight.reshape(mod_weight.shape[0], 3 * local_width),
        preferred_element_type=jnp.float32,
    )
    modulation = modulation.astype(jnp.bfloat16).reshape(frames, 3, local_width)
    whole_rows, whole_mod = (
        lax.all_gather(latents, "ha", axis=2, tiled=True),
        lax.all_gather(modulation[:, :2], "ha", axis=2, tiled=True),
    )
    whole_mod = whole_mod.astype(jnp.float32)
    latent_wide = whole_rows.astype(jnp.float32)
    row_mean = jnp.mean(latent_wide, axis=-1, keepdims=True)
    centered = latent_wide - row_mean
    row_var = jnp.mean(centered * centered, axis=-1, keepdims=True)
    normed = centered * lax.rsqrt(row_var + 1e-06)
    hidden = normed * (1.0 + whole_mod[:, 1][:, None, :]) + whole_mod[:, 0][:, None, :]
    hidden = hidden.astype(jnp.bfloat16).reshape(row_count, full_width)
    projected = jnp.dot(
        hidden, qkv_weight.reshape(full_width, 3 * local_width), preferred_element_type=jnp.float32
    )
    projected = projected.reshape(row_count, 3, head_local, head_size)
    queries = (unit_rms(projected[:, 0]) / math.sqrt(head_size)).astype(jnp.bfloat16)
    key_rows = (
        unit_rms(projected[:, 1]).astype(jnp.bfloat16).reshape(frames, tok_count, local_width)
    )
    value_rows = projected[:, 2].astype(jnp.bfloat16).reshape(frames, tok_count, local_width)
    start_carry = (
        jnp.zeros((row_count, head_local, head_size), jnp.float32),
        jnp.zeros((head_local, row_count), jnp.float32),
    )
    key_all, value_all = (
        lax.all_gather(key_rows, "pb", axis=0, tiled=True),
        lax.all_gather(value_rows, "pb", axis=0, tiled=True),
    )
    numerator, denominator = absorb(start_carry, (key_all, value_all), queries, head_local)
    attended = (
        (numerator / denominator.T[:, :, None]).astype(jnp.bfloat16).reshape(row_count, local_width)
    )
    branch = jnp.dot(
        lax.all_gather(attended, "ha", axis=1, tiled=True),
        out_columns,
        preferred_element_type=jnp.float32,
    )
    branch = branch.reshape(frames, tok_count, local_width)
    gate_wide = modulation[:, 2].astype(jnp.float32)[:, None, :]
    advanced = (latents.astype(jnp.float32) + gate_wide * branch).astype(jnp.bfloat16)
    incoming = from_behind(advanced, "pb", -1)
    is_last = lax.axis_index("pb") == lax.axis_size("pb") - 1
    tail_frame = jnp.where(is_last, noise_frame[None], incoming)
    queue_next = jnp.concatenate([advanced[1:], tail_frame], axis=0)
    return (advanced, queue_next)


EXTRA = 16
LN_ROWS = 16
CHUNKS = 4
MESH = pl.DeviceIdType.MESH
F32 = jnp.float32
BF16 = jnp.bfloat16


def pick(table, index):
    value = jnp.int32(table[0])
    for i in range(1, len(table)):
        value = jnp.where(index == i, jnp.int32(table[i]), value)
    return value


def frame_order(size):
    orders = []
    for z in range(size):
        order = [z]
        for d in range(1, size):
            order += [f for f in (z + d, z - d) if 0 <= f < size]
        orders.append(order)
    return orders


def block_kernel(
    size,
    emb_ref,
    lat_hbm,
    modw_hbm,
    w_hbm,
    wo_hbm,
    noise_hbm,
    adv_hbm,
    next_hbm,
    lat,
    modw,
    w,
    wo,
    hid,
    mods,
    gate,
    qbuf,
    num,
    den,
    own,
    xpart,
    sbuf,
    rbuf,
    xbuf,
    xrecv,
    adv,
    nxt,
    load_sem,
    left_sem,
    right_sem,
    xs_sem,
    ss_sem,
    zr_sem,
    xr_sem,
    sr_sem,
    tail_ss,
    tail_sr,
    tail_xs,
    tail_xr,
    tail_zs,
    tail_zr,
    adv_sem,
    nxt_sem,
):
    z = lax.axis_index("pb")
    h = lax.axis_index("ha")
    core = lax.rem(h, 2)
    sib = h + 1 - 2 * core
    xp = lax.rem(h + 2, 4)
    far = 3 - h
    tok = lat_hbm.shape[1]
    wid = lat_hbm.shape[2]
    full = 4 * wid
    pairs = wid // (2 * HD)
    rows = tok // CHUNKS
    has_left = z > 0
    has_right = z < size - 1

    load_lat = pltpu.make_async_copy(
        lat_hbm.at[0], lat.at[z, h, pl.ds(0, tok)], load_sem.at[0]
    )
    load_modw = pltpu.make_async_copy(modw_hbm, modw, load_sem.at[1])
    load_w = pltpu.make_async_copy(w_hbm, w, load_sem.at[2])
    load_wo = pltpu.make_async_copy(wo_hbm, wo, load_sem.at[3])
    move_noise = pltpu.make_async_copy(noise_hbm, next_hbm.at[0], load_sem.at[4])
    load_modw.start()
    load_lat.start()

    barrier = pltpu.get_barrier_semaphore()
    pl.semaphore_signal(barrier, inc=1, device_id={"ha": sib}, device_id_type=MESH)
    pl.semaphore_signal(barrier, inc=1, device_id={"ha": xp}, device_id_type=MESH)

    @pl.when(has_left)
    def _():
        pl.semaphore_signal(barrier, inc=1, device_id={"pb": z - 1}, device_id_type=MESH)

    @pl.when(has_right)
    def _():
        pl.semaphore_signal(barrier, inc=1, device_id={"pb": z + 1}, device_id_type=MESH)

    load_modw.wait()
    gate_row = None
    lines = []
    for j in range(3):
        made = jnp.dot(emb_ref[...], modw[j], preferred_element_type=F32).astype(BF16)
        lines.append(made.astype(F32))
    gate[...] = lines[2][0:8]
    row_id = lax.broadcasted_iota(jnp.int32, (EXTRA, wid), 0)
    lat[z, h, pl.ds(tok, EXTRA), :] = jnp.where(row_id == 0, lines[0], lines[1]).astype(BF16)
    load_lat.wait()

    waits = 2 + has_left.astype(jnp.int32) + has_right.astype(jnp.int32)
    pl.semaphore_wait(barrier, waits)

    def to_left(f):
        return pltpu.make_async_remote_copy(
            lat.at[f, h], lat.at[f, h], left_sem.at[f], zr_sem.at[f], {"pb": z - 1}, MESH
        )

    def to_right(f):
        return pltpu.make_async_remote_copy(
            lat.at[f, h], lat.at[f, h], right_sem.at[f], zr_sem.at[f], {"pb": z + 1}, MESH
        )

    def to_x(f):
        return pltpu.make_async_remote_copy(
            lat.at[f, h], lat.at[f, h], xs_sem.at[f], xr_sem.at[f], {"ha": xp}, MESH
        )

    def from_x(f):
        return pltpu.make_async_remote_copy(
            lat.at[f, h], lat.at[f, xp], xs_sem.at[f], xr_sem.at[f], {"ha": xp}, MESH
        )

    def to_sib(f, which):
        quarter = h if which == 0 else xp
        return pltpu.make_async_remote_copy(
            lat.at[f, quarter],
            lat.at[f, quarter],
            ss_sem.at[which, f],
            sr_sem.at[which, f],
            {"ha": sib},
            MESH,
        )

    def from_sib(f, which):
        quarter = sib if which == 0 else far
        return pltpu.make_async_remote_copy(
            lat.at[f, quarter],
            lat.at[f, quarter],
            ss_sem.at[which, f],
            sr_sem.at[which, f],
            {"ha": sib},
            MESH,
        )

    @pl.when(has_left)
    def _():
        to_left(z).start()

    @pl.when(has_right)
    def _():
        to_right(z).start()

    to_x(z).start()
    to_sib(z, 0).start()
    load_w.start()
    load_wo.start()

    @pl.when(z == size - 1)
    def _():
        move_noise.start()

    num[...] = jnp.zeros_like(num)
    den[...] = jnp.zeros_like(den)

    orders = frame_order(size)
    load_w.wait()

    def step(s, carry):
        d = s + 1

        @pl.when(z + d < size)
        def _():
            f = z + d
            to_right(f).wait_recv()

            @pl.when(has_left)
            def _():
                to_left(f).start()

            to_x(f).start()
            to_sib(f, 0).start()

        @pl.when(z - d >= 0)
        def _():
            f = z - d
            to_left(f).wait_recv()

            @pl.when(has_right)
            def _():
                to_right(f).start()

            to_x(f).start()
            to_sib(f, 0).start()

        f = jnp.int32(0)
        for i in range(size):
            f = jnp.where(s == i, pick([o[i] for o in orders], z), f)
        from_x(f).wait_recv()
        to_sib(f, 1).start()
        from_sib(f, 0).wait_recv()
        from_sib(f, 1).wait_recv()

        for q in range(4):
            extra = lat[f, q, pl.ds(tok, EXTRA), :].astype(F32)
            mods[0, :, q * wid : (q + 1) * wid] = jnp.broadcast_to(extra[0:1], (8, wid))
            mods[1, :, q * wid : (q + 1) * wid] = jnp.broadcast_to(1.0 + extra[1:2], (8, wid))

        def norm_rows(t, inner):
            r = pl.ds(pl.multiple_of(t * LN_ROWS, LN_ROWS), LN_ROWS)
            parts = [lat[f, q, r, :].astype(F32) for q in range(4)]
            total = parts[0] + parts[1] + parts[2] + parts[3]
            mean = jnp.sum(total, axis=-1, keepdims=True) * (1.0 / full)
            parts = [part - mean for part in parts]
            squares = parts[0] * parts[0]
            for part in parts[1:]:
                squares = squares + part * part
            var = jnp.sum(squares, axis=-1, keepdims=True) * (1.0 / full)
            scale = lax.rsqrt(var + 1e-06)
            for q in range(4):
                cols = slice(q * wid, (q + 1) * wid)
                out = parts[q] * scale * mods[1, 0:1, cols] + mods[0, 0:1, cols]
                hid[r, cols] = out.astype(BF16)
            return inner

        lax.fori_loop(0, tok // LN_ROWS, norm_rows, 0)

        def one_pair(p, inner):
            cols = pl.ds(pl.multiple_of(p * 2 * HD, 2 * HD), 2 * HD)

            @pl.when(s == 0)
            def _():
                q2 = jnp.dot(hid[...], w[0, :, cols], preferred_element_type=F32)
                halves = [
                    unit_rms(q2[:, i * HD : (i + 1) * HD]) / math.sqrt(HD) for i in range(2)
                ]
                qbuf[:, cols] = jnp.concatenate(halves, axis=1).astype(BF16)

            k2 = jnp.dot(hid[...], w[1, :, cols], preferred_element_type=F32)
            keys = [unit_rms(k2[:, i * HD : (i + 1) * HD]).astype(BF16) for i in range(2)]
            values = jnp.dot(hid[...], w[2, :, cols], preferred_element_type=F32).astype(BF16)
            for i in range(2):
                head = pl.ds(pl.multiple_of(p * 2 * HD + i * HD, HD), HD)
                scores = lax.dot_general(
                    qbuf[:, head], keys[i], (((1,), (1,)), ((), ())), preferred_element_type=F32
                )
                weights = jnp.exp(scores)
                den[:, head] += jnp.broadcast_to(
                    jnp.sum(weights, axis=1, keepdims=True), (tok, HD)
                )
                num[:, head] += jnp.dot(
                    weights.astype(BF16),
                    values[:, i * HD : (i + 1) * HD],
                    preferred_element_type=F32,
                )
            return inner

        lax.fori_loop(0, pairs, one_pair, 0)
        return carry

    lax.fori_loop(0, size, step, 0)
    load_wo.wait()

    def chunk(r):
        return pl.ds(pl.multiple_of(r * rows, rows), rows)

    def sib_copy(r):
        return pltpu.make_async_remote_copy(
            sbuf.at[r], rbuf.at[r], tail_ss.at[r], tail_sr.at[r], {"ha": sib}, MESH
        )

    def x_copy(r):
        return pltpu.make_async_remote_copy(
            xbuf.at[r], xrecv.at[r], tail_xs.at[r], tail_xr.at[r], {"ha": xp}, MESH
        )

    def z_send(r):
        return pltpu.make_async_remote_copy(
            adv.at[r], nxt.at[r], tail_zs.at[r], tail_zr.at[r], {"pb": z - 1}, MESH
        )

    def z_recv(r):
        return pltpu.make_async_remote_copy(
            adv.at[r], nxt.at[r], tail_zs.at[r], tail_zr.at[r], {"pb": z + 1}, MESH
        )

    def adv_out(r):
        return pltpu.make_async_copy(adv.at[r], adv_hbm.at[0, chunk(r)], adv_sem.at[r])

    def nxt_out(r):
        return pltpu.make_async_copy(nxt.at[r], next_hbm.at[0, chunk(r)], nxt_sem.at[r])

    def project(att, quarter):
        cols = pl.ds(pl.multiple_of(quarter * wid, wid), wid)
        return jnp.dot(att, wo[:, cols], preferred_element_type=F32)

    def partials(t, carry):
        @pl.when(t < CHUNKS)
        def _():
            att = (num[chunk(t), :] / den[chunk(t), :]).astype(BF16)
            sbuf[t, 1] = project(att, far).astype(BF16)
            sbuf[t, 0] = project(att, sib).astype(BF16)
            sib_copy(t).start()
            xpart[t] = project(att, xp)
            own[t] = project(att, h)

        @pl.when(t >= 1)
        def _():
            r = t - 1
            sib_copy(r).wait_recv()
            xbuf[r] = (xpart[r] + rbuf[r, 1].astype(F32)).astype(BF16)
            x_copy(r).start()

        return carry

    lax.fori_loop(0, CHUNKS + 1, partials, 0)

    def finish(r, carry):
        x_copy(r).wait_recv()
        branch = own[r] + rbuf[r, 0].astype(F32) + xrecv[r].astype(F32)
        latent = lat[z, h, chunk(r), :].astype(F32)
        adv[r] = (latent + gate[0:1] * branch).astype(BF16)

        @pl.when(has_left)
        def _():
            z_send(r).start()

        adv_out(r).start()
        return carry

    lax.fori_loop(0, CHUNKS, finish, 0)

    def drain_frames(f, carry):
        to_x(f).wait_send()
        to_sib(f, 0).wait_send()
        to_sib(f, 1).wait_send()

        @pl.when(has_left & (f >= z))
        def _():
            to_left(f).wait_send()

        @pl.when(has_right & (f <= z))
        def _():
            to_right(f).wait_send()

        return carry

    lax.fori_loop(0, size, drain_frames, 0)

    def take_next(r, carry):
        @pl.when(has_right)
        def _():
            z_recv(r).wait_recv()
            nxt_out(r).start()

        return carry

    lax.fori_loop(0, CHUNKS, take_next, 0)

    def drain_tail(r, carry):
        sib_copy(r).wait_send()
        x_copy(r).wait_send()
        adv_out(r).wait()

        @pl.when(has_left)
        def _():
            z_send(r).wait_send()

        @pl.when(has_right)
        def _():
            nxt_out(r).wait()

        return carry

    lax.fori_loop(0, CHUNKS, drain_tail, 0)

    @pl.when(z == size - 1)
    def _():
        move_noise.wait()


def fused(size, latents, timesteps, mod_weight, qkv_weight, out_weight, noise_frame):
    _, tok, wid = latents.shape
    full = 4 * wid
    rows = tok // CHUNKS
    embedding = sinusoid(timesteps).astype(BF16)
    embedding = jnp.broadcast_to(embedding, (EXTRA, TDIM))
    anywhere = pl.BlockSpec(memory_space=pl.ANY)
    dma = pltpu.SemaphoreType.DMA
    flops = 2 * tok * full * wid * (1 + 2 * size) + 4 * tok * tok * size * wid + 2 * tok * wid * full
    return pl.pallas_call(
        functools.partial(block_kernel, size),
        out_shape=(
            jax.ShapeDtypeStruct(latents.shape, BF16),
            jax.ShapeDtypeStruct(latents.shape, BF16),
        ),
        in_specs=[pl.BlockSpec(memory_space=pltpu.VMEM)] + [anywhere] * 5,
        out_specs=(anywhere, anywhere),
        scratch_shapes=[
            pltpu.VMEM((size, 4, tok + EXTRA, wid), BF16),
            pltpu.VMEM((3, TDIM, wid), BF16),
            pltpu.VMEM((3, full, wid), BF16),
            pltpu.VMEM((wid, full), BF16),
            pltpu.VMEM((tok, full), BF16),
            pltpu.VMEM((2, 8, full), F32),
            pltpu.VMEM((8, wid), F32),
            pltpu.VMEM((tok, wid), BF16),
            pltpu.VMEM((tok, wid), F32),
            pltpu.VMEM((tok, wid), F32),
            pltpu.VMEM((CHUNKS, rows, wid), F32),
            pltpu.VMEM((CHUNKS, rows, wid), F32),
            pltpu.VMEM((CHUNKS, 2, rows, wid), BF16),
            pltpu.VMEM((CHUNKS, 2, rows, wid), BF16),
            pltpu.VMEM((CHUNKS, rows, wid), BF16),
            pltpu.VMEM((CHUNKS, rows, wid), BF16),
            pltpu.VMEM((CHUNKS, rows, wid), BF16),
            pltpu.VMEM((CHUNKS, rows, wid), BF16),
            dma((5,)),
            dma((size,)),
            dma((size,)),
            dma((size,)),
            dma((2, size)),
            dma((size,)),
            dma((size,)),
            dma((2, size)),
            dma((CHUNKS,)),
            dma((CHUNKS,)),
            dma((CHUNKS,)),
            dma((CHUNKS,)),
            dma((CHUNKS,)),
            dma((CHUNKS,)),
            dma((CHUNKS,)),
            dma((CHUNKS,)),
        ],
        compiler_params=pltpu.CompilerParams(
            collective_id=0, has_side_effects=True, vmem_limit_bytes=58 * 1024 * 1024
        ),
        cost_estimate=pl.CostEstimate(
            flops=flops, bytes_accessed=22_000_000, transcendentals=tok * tok * size * wid // HD
        ),
    )(
        embedding,
        latents,
        mod_weight.transpose(1, 0, 2),
        qkv_weight.transpose(1, 0, 2),
        out_weight,
        noise_frame,
    )


def solution(mesh):
    placed = (
        P(("grp", "pb"), None, "ha"),
        P(("grp", "pb")),
        P(None, None, "ha"),
        P(None, None, "ha"),
        P("ha", None),
        P("grp", "ha"),
    )
    small = mesh.shape["ha"] == 4 and mesh.shape["pb"] <= 4
    return jax.shard_map(
        functools.partial(fused, mesh.shape["pb"]) if small else on_device,
        mesh=mesh,
        in_specs=placed,
        out_specs=(P(("grp", "pb"), None, "ha"), P(("grp", "pb"), None, "ha")),
        check_vma=False,
    )
```

```python
import functools
import math

import jax
import jax.numpy as jnp
from jax import lax
from jax.experimental import pallas as pl
from jax.experimental.pallas import tpu as pltpu
from jax.sharding import PartitionSpec as P

HD = 128
TDIM = 256


def from_behind(x, axis, by):
    size = lax.axis_size(axis)
    pairs = [(i, i + by) for i in range(size) if 0 <= i + by < size]
    return lax.ppermute(x, axis, pairs)


def sinusoid(timesteps):
    half_width = TDIM // 2
    frequency = jnp.exp(-math.log(10000.0) * jnp.arange(half_width, dtype=jnp.float32) / half_width)
    angles = timesteps.astype(jnp.float32)[:, None] * frequency[None, :]
    return jnp.concatenate([jnp.cos(angles), jnp.sin(angles)], axis=1)


def unit_rms(vectors):
    return vectors * lax.rsqrt(jnp.mean(vectors * vectors, axis=-1, keepdims=True) + 1e-06)


def absorb(running, pieces, queries, head_local):
    key_piece, value_piece = pieces

    def one_frame(position, inner):
        numerator, denominator = inner
        key_frame = lax.dynamic_index_in_dim(key_piece, position, 0, keepdims=False)
        value_frame = lax.dynamic_index_in_dim(value_piece, position, 0, keepdims=False)
        key_count = key_frame.shape[0]
        key_frame = key_frame.reshape(key_count, head_local, -1)
        value_frame = value_frame.reshape(key_count, head_local, -1)
        scores = jnp.einsum("rhd,khd->hrk", queries, key_frame, preferred_element_type=jnp.float32)
        weights_exp = jnp.exp(scores)
        denominator = denominator + jnp.sum(weights_exp, axis=2)
        numerator = numerator + jnp.einsum(
            "hrk,khd->rhd",
            weights_exp.astype(jnp.bfloat16),
            value_frame,
            preferred_element_type=jnp.float32,
        )
        return (numerator, denominator)

    return lax.fori_loop(0, key_piece.shape[0], one_frame, running)


def on_device(latents, timesteps, mod_weight, qkv_weight, out_weight, noise_frame):
    frames, tok_count, local_width = latents.shape
    full_width = qkv_weight.shape[0]
    head_size = HD
    head_local = local_width // head_size
    row_count = frames * tok_count
    out_columns = lax.all_to_all(out_weight, "ha", split_axis=1, concat_axis=0, tiled=True)
    embedding = sinusoid(timesteps).astype(jnp.bfloat16)
    modulation = jnp.dot(
        embedding,
        mod_weight.reshape(mod_weight.shape[0], 3 * local_width),
        preferred_element_type=jnp.float32,
    )
    modulation = modulation.astype(jnp.bfloat16).reshape(frames, 3, local_width)
    whole_rows, whole_mod = (
        lax.all_gather(latents, "ha", axis=2, tiled=True),
        lax.all_gather(modulation[:, :2], "ha", axis=2, tiled=True),
    )
    whole_mod = whole_mod.astype(jnp.float32)
    latent_wide = whole_rows.astype(jnp.float32)
    row_mean = jnp.mean(latent_wide, axis=-1, keepdims=True)
    centered = latent_wide - row_mean
    row_var = jnp.mean(centered * centered, axis=-1, keepdims=True)
    normed = centered * lax.rsqrt(row_var + 1e-06)
    hidden = normed * (1.0 + whole_mod[:, 1][:, None, :]) + whole_mod[:, 0][:, None, :]
    hidden = hidden.astype(jnp.bfloat16).reshape(row_count, full_width)
    projected = jnp.dot(
        hidden, qkv_weight.reshape(full_width, 3 * local_width), preferred_element_type=jnp.float32
    )
    projected = projected.reshape(row_count, 3, head_local, head_size)
    queries = (unit_rms(projected[:, 0]) / math.sqrt(head_size)).astype(jnp.bfloat16)
    key_rows = (
        unit_rms(projected[:, 1]).astype(jnp.bfloat16).reshape(frames, tok_count, local_width)
    )
    value_rows = projected[:, 2].astype(jnp.bfloat16).reshape(frames, tok_count, local_width)
    start_carry = (
        jnp.zeros((row_count, head_local, head_size), jnp.float32),
        jnp.zeros((head_local, row_count), jnp.float32),
    )
    key_all, value_all = (
        lax.all_gather(key_rows, "pb", axis=0, tiled=True),
        lax.all_gather(value_rows, "pb", axis=0, tiled=True),
    )
    numerator, denominator = absorb(start_carry, (key_all, value_all), queries, head_local)
    attended = (
        (numerator / denominator.T[:, :, None]).astype(jnp.bfloat16).reshape(row_count, local_width)
    )
    branch = jnp.dot(
        lax.all_gather(attended, "ha", axis=1, tiled=True),
        out_columns,
        preferred_element_type=jnp.float32,
    )
    branch = branch.reshape(frames, tok_count, local_width)
    gate_wide = modulation[:, 2].astype(jnp.float32)[:, None, :]
    advanced = (latents.astype(jnp.float32) + gate_wide * branch).astype(jnp.bfloat16)
    incoming = from_behind(advanced, "pb", -1)
    is_last = lax.axis_index("pb") == lax.axis_size("pb") - 1
    tail_frame = jnp.where(is_last, noise_frame[None], incoming)
    queue_next = jnp.concatenate([advanced[1:], tail_frame], axis=0)
    return (advanced, queue_next)


EXTRA = 16
LN_ROWS = 16
CHUNKS = 4
MESH = pl.DeviceIdType.MESH
F32 = jnp.float32
BF16 = jnp.bfloat16


def pick(table, index):
    value = jnp.int32(table[0])
    for i in range(1, len(table)):
        value = jnp.where(index == i, jnp.int32(table[i]), value)
    return value


def frame_order(size):
    orders = []
    for z in range(size):
        order = [z]
        for d in range(1, size):
            order += [f for f in (z + d, z - d) if 0 <= f < size]
        orders.append(order)
    return orders


def block_kernel(
    size,
    emb_ref,
    lat_hbm,
    modw_hbm,
    w_hbm,
    wo_hbm,
    noise_hbm,
    adv_hbm,
    next_hbm,
    lat,
    modw,
    w,
    wo,
    hid,
    mods,
    gate,
    qbuf,
    num,
    den,
    own,
    xpart,
    sbuf,
    rbuf,
    xbuf,
    xrecv,
    adv,
    nxt,
    load_sem,
    left_sem,
    right_sem,
    xs_sem,
    ss_sem,
    zr_sem,
    xr_sem,
    sr_sem,
    tail_ss,
    tail_sr,
    tail_xs,
    tail_xr,
    tail_zs,
    tail_zr,
    adv_sem,
    nxt_sem,
):
    z = lax.axis_index("pb")
    h = lax.axis_index("ha")
    core = lax.rem(h, 2)
    sib = h + 1 - 2 * core
    xp = lax.rem(h + 2, 4)
    far = 3 - h
    tok = lat_hbm.shape[1]
    wid = lat_hbm.shape[2]
    full = 4 * wid
    pairs = wid // (2 * HD)
    rows = tok // CHUNKS
    has_left = z > 0
    has_right = z < size - 1

    load_lat = pltpu.make_async_copy(
        lat_hbm.at[0], lat.at[z, h, pl.ds(EXTRA, tok)], load_sem.at[0]
    )
    load_modw = pltpu.make_async_copy(modw_hbm, modw, load_sem.at[1])
    load_w = pltpu.make_async_copy(w_hbm, w, load_sem.at[2])
    load_wo = pltpu.make_async_copy(wo_hbm, wo, load_sem.at[3])
    move_noise = pltpu.make_async_copy(noise_hbm, next_hbm.at[0], load_sem.at[4])
    load_modw.start()
    load_lat.start()

    barrier = pltpu.get_barrier_semaphore()
    pl.semaphore_signal(barrier, inc=1, device_id={"ha": sib}, device_id_type=MESH)
    pl.semaphore_signal(barrier, inc=1, device_id={"ha": xp}, device_id_type=MESH)

    @pl.when(has_left)
    def _():
        pl.semaphore_signal(barrier, inc=1, device_id={"pb": z - 1}, device_id_type=MESH)

    @pl.when(has_right)
    def _():
        pl.semaphore_signal(barrier, inc=1, device_id={"pb": z + 1}, device_id_type=MESH)

    load_modw.wait()
    lines = []
    for j in range(3):
        made = jnp.dot(emb_ref[...], modw[j], preferred_element_type=F32).astype(BF16)
        lines.append(made.astype(F32))
    gate[...] = lines[2][0:8]
    row_id = lax.broadcasted_iota(jnp.int32, (EXTRA, wid), 0)
    lat[z, h, pl.ds(0, EXTRA), :] = jnp.where(row_id == 0, lines[0], lines[1]).astype(BF16)
    load_lat.wait()

    waits = 2 + has_left.astype(jnp.int32) + has_right.astype(jnp.int32)
    pl.semaphore_wait(barrier, waits)

    half = tok // 2
    spans = (pl.ds(0, EXTRA + half), pl.ds(EXTRA + half, half))

    def remote(f, m, quarter, send, recv, device):
        ref = lat.at[f, quarter, spans[m]]
        return pltpu.make_async_remote_copy(ref, ref, send.at[m, f], recv.at[m, f], device, MESH)

    def to_left(f, m):
        return remote(f, m, h, left_sem, zr_sem, {"pb": z - 1})

    def to_right(f, m):
        return remote(f, m, h, right_sem, zr_sem, {"pb": z + 1})

    def to_x(f, m):
        return remote(f, m, h, xs_sem, xr_sem, {"ha": xp})

    def from_x(f, m):
        return remote(f, m, xp, xs_sem, xr_sem, {"ha": xp})

    def to_sib(f, m, which):
        quarter = h if which == 0 else xp
        return remote(f, m, quarter, ss_sem.at[which], sr_sem.at[which], {"ha": sib})

    def from_sib(f, m, which):
        quarter = sib if which == 0 else far
        return remote(f, m, quarter, ss_sem.at[which], sr_sem.at[which], {"ha": sib})

    for m in range(2):

        @pl.when(has_left)
        def _():
            to_left(z, m).start()

        @pl.when(has_right)
        def _():
            to_right(z, m).start()

        to_x(z, m).start()
        to_sib(z, m, 0).start()
    load_w.start()
    load_wo.start()

    @pl.when(z == size - 1)
    def _():
        move_noise.start()

    num[...] = jnp.zeros_like(num)
    den[...] = jnp.zeros_like(den)

    def forward(k):
        d, m = k // 2 + 1, k % 2

        @pl.when(z + d < size)
        def _():
            f = z + d
            to_right(f, m).wait_recv()

            @pl.when(has_left)
            def _():
                to_left(f, m).start()

            to_x(f, m).start()
            to_sib(f, m, 0).start()

        @pl.when(z - d >= 0)
        def _():
            f = z - d
            to_left(f, m).wait_recv()

            @pl.when(has_right)
            def _():
                to_right(f, m).start()

            to_x(f, m).start()
            to_sib(f, m, 0).start()

    def norm_unit(f, m):
        from_x(f, m).wait_recv()
        to_sib(f, m, 1).start()
        from_sib(f, m, 0).wait_recv()
        from_sib(f, m, 1).wait_recv()
        if m == 0:
            for q in range(4):
                cols = slice(q * wid, (q + 1) * wid)
                extra = lat[f, q, pl.ds(0, EXTRA), :].astype(F32)
                mods[0, :, cols] = jnp.broadcast_to(extra[0:1], (8, wid))
                mods[1, :, cols] = jnp.broadcast_to(1.0 + extra[1:2], (8, wid))

        def norm_rows(t, inner):
            r = pl.ds(pl.multiple_of(t * LN_ROWS + m * half, LN_ROWS), LN_ROWS)
            src = pl.ds(pl.multiple_of(t * LN_ROWS + m * half + EXTRA, LN_ROWS), LN_ROWS)
            parts = [lat[f, q, src, :].astype(F32) for q in range(4)]
            total = parts[0] + parts[1] + parts[2] + parts[3]
            mean = jnp.sum(total, axis=-1, keepdims=True) * (1.0 / full)
            parts = [part - mean for part in parts]
            squares = parts[0] * parts[0]
            for part in parts[1:]:
                squares = squares + part * part
            var = jnp.sum(squares, axis=-1, keepdims=True) * (1.0 / full)
            scale = lax.rsqrt(var + 1e-06)
            for q in range(4):
                cols = slice(q * wid, (q + 1) * wid)
                out = parts[q] * scale * mods[1, 0:1, cols] + mods[0, 0:1, cols]
                hid[r, cols] = out.astype(BF16)
            return inner

        lax.fori_loop(0, half // LN_ROWS, norm_rows, 0, unroll=4)

    def absorb_rows(rows, first):
        def one_pair(p, inner):
            cols = pl.ds(pl.multiple_of(p * 2 * HD, 2 * HD), 2 * HD)
            if first:

                @pl.when(p == 1)
                def _():
                    forward(2)

                q2 = jnp.dot(hid[...], w[0, :, cols], preferred_element_type=F32)
                halves = [
                    unit_rms(q2[:, i * HD : (i + 1) * HD]) / math.sqrt(HD) for i in range(2)
                ]
                qbuf[:, cols] = jnp.concatenate(halves, axis=1).astype(BF16)

            k2 = jnp.dot(hid[rows, :], w[1, :, cols], preferred_element_type=F32)
            keys = [unit_rms(k2[:, i * HD : (i + 1) * HD]).astype(BF16) for i in range(2)]
            values = jnp.dot(hid[rows, :], w[2, :, cols], preferred_element_type=F32).astype(BF16)
            for i in range(2):
                head = pl.ds(pl.multiple_of(p * 2 * HD + i * HD, HD), HD)
                scores = lax.dot_general(
                    qbuf[:, head], keys[i], (((1,), (1,)), ((), ())), preferred_element_type=F32
                )
                weights = jnp.exp(scores)
                den[:, head] += jnp.broadcast_to(
                    jnp.sum(weights, axis=1, keepdims=True), (tok, HD)
                )
                num[:, head] += jnp.dot(
                    weights.astype(BF16),
                    values[:, i * HD : (i + 1) * HD],
                    preferred_element_type=F32,
                )
            return inner

        lax.fori_loop(0, pairs, one_pair, 0)

    orders = frame_order(size)
    forward(0)
    norm_unit(z, 0)
    forward(1)
    norm_unit(z, 1)
    load_w.wait()
    absorb_rows(slice(0, tok), True)

    def step(s, carry):
        f = jnp.int32(0)
        for i in range(1, size):
            f = jnp.where(s == i, pick([o[i] for o in orders], z), f)
        norm_unit(f, 0)

        @pl.when(s == 1)
        def _():
            forward(3)

        absorb_rows(slice(0, half), False)
        norm_unit(f, 1)

        @pl.when(s == 2)
        def _():
            forward(5)

        absorb_rows(slice(half, tok), False)

        @pl.when(s == 1)
        def _():
            forward(4)

        return carry

    lax.fori_loop(1, size, step, 0)
    load_wo.wait()

    def chunk(r):
        return pl.ds(pl.multiple_of(r * rows, rows), rows)

    def token_rows(r):
        return pl.ds(pl.multiple_of(r * rows + EXTRA, LN_ROWS), rows)

    def sib_copy(r):
        return pltpu.make_async_remote_copy(
            sbuf.at[r], rbuf.at[r], tail_ss.at[r], tail_sr.at[r], {"ha": sib}, MESH
        )

    def x_copy(r):
        return pltpu.make_async_remote_copy(
            xbuf.at[r], xrecv.at[r], tail_xs.at[r], tail_xr.at[r], {"ha": xp}, MESH
        )

    def z_send(r):
        return pltpu.make_async_remote_copy(
            adv.at[r], nxt.at[r], tail_zs.at[r], tail_zr.at[r], {"pb": z - 1}, MESH
        )

    def z_recv(r):
        return pltpu.make_async_remote_copy(
            adv.at[r], nxt.at[r], tail_zs.at[r], tail_zr.at[r], {"pb": z + 1}, MESH
        )

    def adv_out(r):
        return pltpu.make_async_copy(adv.at[r], adv_hbm.at[0, chunk(r)], adv_sem.at[r])

    def nxt_out(r):
        return pltpu.make_async_copy(nxt.at[r], next_hbm.at[0, chunk(r)], nxt_sem.at[r])

    def project(att, quarter):
        cols = pl.ds(pl.multiple_of(quarter * wid, wid), wid)
        return jnp.dot(att, wo[:, cols], preferred_element_type=F32)

    def partials(t, carry):
        @pl.when(t < CHUNKS)
        def _():
            att = (num[chunk(t), :] / den[chunk(t), :]).astype(BF16)
            sbuf[t, 1] = project(att, far).astype(BF16)
            sbuf[t, 0] = project(att, sib).astype(BF16)
            sib_copy(t).start()
            xpart[t] = project(att, xp)
            own[t] = project(att, h)

        @pl.when(t >= 1)
        def _():
            r = t - 1
            sib_copy(r).wait_recv()
            xbuf[r] = (xpart[r] + rbuf[r, 1].astype(F32)).astype(BF16)
            x_copy(r).start()

        return carry

    lax.fori_loop(0, CHUNKS + 1, partials, 0)

    def finish(r, carry):
        x_copy(r).wait_recv()
        branch = own[r] + rbuf[r, 0].astype(F32) + xrecv[r].astype(F32)
        latent = lat[z, h, token_rows(r), :].astype(F32)
        adv[r] = (latent + gate[0:1] * branch).astype(BF16)

        @pl.when(has_left)
        def _():
            z_send(r).start()

        adv_out(r).start()
        return carry

    lax.fori_loop(0, CHUNKS, finish, 0)

    def drain_frames(f, carry):
        for m in range(2):
            to_x(f, m).wait_send()
            to_sib(f, m, 0).wait_send()
            to_sib(f, m, 1).wait_send()

            @pl.when(has_left & (f >= z))
            def _():
                to_left(f, m).wait_send()

            @pl.when(has_right & (f <= z))
            def _():
                to_right(f, m).wait_send()

        return carry

    lax.fori_loop(0, size, drain_frames, 0)

    def take_next(r, carry):
        @pl.when(has_right)
        def _():
            z_recv(r).wait_recv()
            nxt_out(r).start()

        return carry

    lax.fori_loop(0, CHUNKS, take_next, 0)

    def drain_tail(r, carry):
        sib_copy(r).wait_send()
        x_copy(r).wait_send()
        adv_out(r).wait()

        @pl.when(has_left)
        def _():
            z_send(r).wait_send()

        @pl.when(has_right)
        def _():
            nxt_out(r).wait()

        return carry

    lax.fori_loop(0, CHUNKS, drain_tail, 0)

    @pl.when(z == size - 1)
    def _():
        move_noise.wait()


def land_kernel(a_ref, b_ref, a_out, b_out):
    a_out[...] = a_ref[...]
    b_out[...] = b_ref[...]


def fused(size, latents, timesteps, mod_weight, qkv_weight, out_weight, noise_frame):
    _, tok, wid = latents.shape
    full = 4 * wid
    rows = tok // CHUNKS
    embedding = sinusoid(timesteps).astype(BF16)
    embedding = jnp.broadcast_to(embedding, (EXTRA, TDIM))
    anywhere = pl.BlockSpec(memory_space=pl.ANY)
    dma = pltpu.SemaphoreType.DMA
    flops = 2 * tok * full * wid * (1 + 2 * size) + 4 * tok * tok * size * wid + 2 * tok * wid * full
    outs = pl.pallas_call(
        functools.partial(block_kernel, size),
        out_shape=(
            jax.ShapeDtypeStruct(latents.shape, BF16),
            jax.ShapeDtypeStruct(latents.shape, BF16),
        ),
        in_specs=[pl.BlockSpec(memory_space=pltpu.VMEM)] + [anywhere] * 5,
        out_specs=(anywhere, anywhere),
        scratch_shapes=[
            pltpu.VMEM((size, 4, tok + EXTRA, wid), BF16),
            pltpu.VMEM((3, TDIM, wid), BF16),
            pltpu.VMEM((3, full, wid), BF16),
            pltpu.VMEM((wid, full), BF16),
            pltpu.VMEM((tok, full), BF16),
            pltpu.VMEM((2, 8, full), F32),
            pltpu.VMEM((8, wid), F32),
            pltpu.VMEM((tok, wid), BF16),
            pltpu.VMEM((tok, wid), F32),
            pltpu.VMEM((tok, wid), F32),
            pltpu.VMEM((CHUNKS, rows, wid), F32),
            pltpu.VMEM((CHUNKS, rows, wid), F32),
            pltpu.VMEM((CHUNKS, 2, rows, wid), BF16),
            pltpu.VMEM((CHUNKS, 2, rows, wid), BF16),
            pltpu.VMEM((CHUNKS, rows, wid), BF16),
            pltpu.VMEM((CHUNKS, rows, wid), BF16),
            pltpu.VMEM((CHUNKS, rows, wid), BF16),
            pltpu.VMEM((CHUNKS, rows, wid), BF16),
            dma((5,)),
            dma((2, size)),
            dma((2, size)),
            dma((2, size)),
            dma((2, 2, size)),
            dma((2, size)),
            dma((2, size)),
            dma((2, 2, size)),
            dma((CHUNKS,)),
            dma((CHUNKS,)),
            dma((CHUNKS,)),
            dma((CHUNKS,)),
            dma((CHUNKS,)),
            dma((CHUNKS,)),
            dma((CHUNKS,)),
            dma((CHUNKS,)),
        ],
        compiler_params=pltpu.CompilerParams(
            collective_id=0, has_side_effects=True, vmem_limit_bytes=58 * 1024 * 1024
        ),
        cost_estimate=pl.CostEstimate(
            flops=flops, bytes_accessed=22_000_000, transcendentals=tok * tok * size * wid // HD
        ),
    )(
        embedding,
        latents,
        mod_weight.transpose(1, 0, 2),
        qkv_weight.transpose(1, 0, 2),
        out_weight,
        noise_frame,
    )
    piece = pl.BlockSpec((1, rows, wid), lambda i: (0, i, 0))
    return pl.pallas_call(
        land_kernel,
        grid=(CHUNKS,),
        out_shape=(
            jax.ShapeDtypeStruct(latents.shape, BF16),
            jax.ShapeDtypeStruct(latents.shape, BF16),
        ),
        in_specs=[piece, piece],
        out_specs=(piece, piece),
    )(*outs)


def solution(mesh):
    placed = (
        P(("grp", "pb"), None, "ha"),
        P(("grp", "pb")),
        P(None, None, "ha"),
        P(None, None, "ha"),
        P("ha", None),
        P("grp", "ha"),
    )
    small = mesh.shape["ha"] == 4 and mesh.shape["pb"] <= 4
    return jax.shard_map(
        functools.partial(fused, mesh.shape["pb"]) if small else on_device,
        mesh=mesh,
        in_specs=placed,
        out_specs=(P(("grp", "pb"), None, "ha"), P(("grp", "pb"), None, "ha")),
        check_vma=False,
    )
```

```python
import functools
import math

import jax
import jax.numpy as jnp
from jax import lax
from jax.experimental import pallas as pl
from jax.experimental.pallas import tpu as pltpu
from jax.sharding import PartitionSpec as P

HD = 128
TDIM = 256


def from_behind(x, axis, by):
    size = lax.axis_size(axis)
    pairs = [(i, i + by) for i in range(size) if 0 <= i + by < size]
    return lax.ppermute(x, axis, pairs)


def sinusoid(timesteps):
    half_width = TDIM // 2
    frequency = jnp.exp(-math.log(10000.0) * jnp.arange(half_width, dtype=jnp.float32) / half_width)
    angles = timesteps.astype(jnp.float32)[:, None] * frequency[None, :]
    return jnp.concatenate([jnp.cos(angles), jnp.sin(angles)], axis=1)


def unit_rms(vectors):
    return vectors * lax.rsqrt(jnp.mean(vectors * vectors, axis=-1, keepdims=True) + 1e-06)


def absorb(running, pieces, queries, head_local):
    key_piece, value_piece = pieces

    def one_frame(position, inner):
        numerator, denominator = inner
        key_frame = lax.dynamic_index_in_dim(key_piece, position, 0, keepdims=False)
        value_frame = lax.dynamic_index_in_dim(value_piece, position, 0, keepdims=False)
        key_count = key_frame.shape[0]
        key_frame = key_frame.reshape(key_count, head_local, -1)
        value_frame = value_frame.reshape(key_count, head_local, -1)
        scores = jnp.einsum("rhd,khd->hrk", queries, key_frame, preferred_element_type=jnp.float32)
        weights_exp = jnp.exp(scores)
        denominator = denominator + jnp.sum(weights_exp, axis=2)
        numerator = numerator + jnp.einsum(
            "hrk,khd->rhd",
            weights_exp.astype(jnp.bfloat16),
            value_frame,
            preferred_element_type=jnp.float32,
        )
        return (numerator, denominator)

    return lax.fori_loop(0, key_piece.shape[0], one_frame, running)


def on_device(latents, timesteps, mod_weight, qkv_weight, out_weight, noise_frame):
    frames, tok_count, local_width = latents.shape
    full_width = qkv_weight.shape[0]
    head_size = HD
    head_local = local_width // head_size
    row_count = frames * tok_count
    out_columns = lax.all_to_all(out_weight, "ha", split_axis=1, concat_axis=0, tiled=True)
    embedding = sinusoid(timesteps).astype(jnp.bfloat16)
    modulation = jnp.dot(
        embedding,
        mod_weight.reshape(mod_weight.shape[0], 3 * local_width),
        preferred_element_type=jnp.float32,
    )
    modulation = modulation.astype(jnp.bfloat16).reshape(frames, 3, local_width)
    whole_rows, whole_mod = (
        lax.all_gather(latents, "ha", axis=2, tiled=True),
        lax.all_gather(modulation[:, :2], "ha", axis=2, tiled=True),
    )
    whole_mod = whole_mod.astype(jnp.float32)
    latent_wide = whole_rows.astype(jnp.float32)
    row_mean = jnp.mean(latent_wide, axis=-1, keepdims=True)
    centered = latent_wide - row_mean
    row_var = jnp.mean(centered * centered, axis=-1, keepdims=True)
    normed = centered * lax.rsqrt(row_var + 1e-06)
    hidden = normed * (1.0 + whole_mod[:, 1][:, None, :]) + whole_mod[:, 0][:, None, :]
    hidden = hidden.astype(jnp.bfloat16).reshape(row_count, full_width)
    projected = jnp.dot(
        hidden, qkv_weight.reshape(full_width, 3 * local_width), preferred_element_type=jnp.float32
    )
    projected = projected.reshape(row_count, 3, head_local, head_size)
    queries = (unit_rms(projected[:, 0]) / math.sqrt(head_size)).astype(jnp.bfloat16)
    key_rows = (
        unit_rms(projected[:, 1]).astype(jnp.bfloat16).reshape(frames, tok_count, local_width)
    )
    value_rows = projected[:, 2].astype(jnp.bfloat16).reshape(frames, tok_count, local_width)
    start_carry = (
        jnp.zeros((row_count, head_local, head_size), jnp.float32),
        jnp.zeros((head_local, row_count), jnp.float32),
    )
    key_all, value_all = (
        lax.all_gather(key_rows, "pb", axis=0, tiled=True),
        lax.all_gather(value_rows, "pb", axis=0, tiled=True),
    )
    numerator, denominator = absorb(start_carry, (key_all, value_all), queries, head_local)
    attended = (
        (numerator / denominator.T[:, :, None]).astype(jnp.bfloat16).reshape(row_count, local_width)
    )
    branch = jnp.dot(
        lax.all_gather(attended, "ha", axis=1, tiled=True),
        out_columns,
        preferred_element_type=jnp.float32,
    )
    branch = branch.reshape(frames, tok_count, local_width)
    gate_wide = modulation[:, 2].astype(jnp.float32)[:, None, :]
    advanced = (latents.astype(jnp.float32) + gate_wide * branch).astype(jnp.bfloat16)
    incoming = from_behind(advanced, "pb", -1)
    is_last = lax.axis_index("pb") == lax.axis_size("pb") - 1
    tail_frame = jnp.where(is_last, noise_frame[None], incoming)
    queue_next = jnp.concatenate([advanced[1:], tail_frame], axis=0)
    return (advanced, queue_next)


EXTRA = 16
LN_ROWS = 16
CHUNKS = 4
MESH = pl.DeviceIdType.MESH
F32 = jnp.float32
BF16 = jnp.bfloat16


def pick(table, index):
    value = jnp.int32(table[0])
    for i in range(1, len(table)):
        value = jnp.where(index == i, jnp.int32(table[i]), value)
    return value


def frame_order(size):
    orders = []
    for z in range(size):
        order = [z]
        for d in range(1, size):
            order += [f for f in (z + d, z - d) if 0 <= f < size]
        orders.append(order)
    return orders


def block_kernel(
    size,
    emb_ref,
    lat_hbm,
    modw_hbm,
    w_hbm,
    wo_hbm,
    noise_hbm,
    adv_hbm,
    next_hbm,
    lat,
    modw,
    w,
    wo,
    hid,
    mods,
    gate,
    qbuf,
    num,
    den,
    own,
    xpart,
    sbuf,
    rbuf,
    xbuf,
    xrecv,
    adv,
    nxt,
    load_sem,
    left_sem,
    right_sem,
    xs_sem,
    ss_sem,
    zr_sem,
    xr_sem,
    sr_sem,
    tail_ss,
    tail_sr,
    tail_xs,
    tail_xr,
    tail_zs,
    tail_zr,
    adv_sem,
    nxt_sem,
):
    z = lax.axis_index("pb")
    h = lax.axis_index("ha")
    core = lax.rem(h, 2)
    sib = h + 1 - 2 * core
    xp = lax.rem(h + 2, 4)
    far = 3 - h
    tok = lat_hbm.shape[1]
    wid = lat_hbm.shape[2]
    full = 4 * wid
    pairs = wid // (2 * HD)
    rows = tok // CHUNKS
    has_left = z > 0
    has_right = z < size - 1

    load_lat = pltpu.make_async_copy(
        lat_hbm.at[0], lat.at[z, h, pl.ds(EXTRA, tok)], load_sem.at[0]
    )
    load_modw = pltpu.make_async_copy(modw_hbm, modw, load_sem.at[1])
    load_w = pltpu.make_async_copy(w_hbm, w, load_sem.at[2])
    load_wo = pltpu.make_async_copy(wo_hbm, wo, load_sem.at[3])
    move_noise = pltpu.make_async_copy(noise_hbm, next_hbm.at[0], load_sem.at[4])
    load_modw.start()
    load_lat.start()

    barrier = pltpu.get_barrier_semaphore()
    pl.semaphore_signal(barrier, inc=1, device_id={"ha": sib}, device_id_type=MESH)
    pl.semaphore_signal(barrier, inc=1, device_id={"ha": xp}, device_id_type=MESH)

    @pl.when(has_left)
    def _():
        pl.semaphore_signal(barrier, inc=1, device_id={"pb": z - 1}, device_id_type=MESH)

    @pl.when(has_right)
    def _():
        pl.semaphore_signal(barrier, inc=1, device_id={"pb": z + 1}, device_id_type=MESH)

    load_modw.wait()
    lines = []
    for j in range(3):
        made = jnp.dot(emb_ref[...], modw[j], preferred_element_type=F32).astype(BF16)
        lines.append(made.astype(F32))
    gate[...] = lines[2][0:8]
    row_id = lax.broadcasted_iota(jnp.int32, (EXTRA, wid), 0)
    lat[z, h, pl.ds(0, EXTRA), :] = jnp.where(row_id == 0, lines[0], lines[1]).astype(BF16)
    load_lat.wait()

    waits = 2 + has_left.astype(jnp.int32) + has_right.astype(jnp.int32)
    pl.semaphore_wait(barrier, waits)

    half = tok // 2
    spans = (pl.ds(0, EXTRA + half), pl.ds(EXTRA + half, half))

    def remote(f, m, quarter, send, recv, device):
        ref = lat.at[f, quarter, spans[m]]
        return pltpu.make_async_remote_copy(ref, ref, send.at[m, f], recv.at[m, f], device, MESH)

    def to_left(f, m):
        return remote(f, m, h, left_sem, zr_sem, {"pb": z - 1})

    def to_right(f, m):
        return remote(f, m, h, right_sem, zr_sem, {"pb": z + 1})

    def to_x(f, m):
        return remote(f, m, h, xs_sem, xr_sem, {"ha": xp})

    def from_x(f, m):
        return remote(f, m, xp, xs_sem, xr_sem, {"ha": xp})

    def to_sib(f, m, which):
        quarter = h if which == 0 else xp
        return remote(f, m, quarter, ss_sem.at[which], sr_sem.at[which], {"ha": sib})

    def from_sib(f, m, which):
        quarter = sib if which == 0 else far
        return remote(f, m, quarter, ss_sem.at[which], sr_sem.at[which], {"ha": sib})

    for m in range(2):

        @pl.when(has_left)
        def _():
            to_left(z, m).start()

        @pl.when(has_right)
        def _():
            to_right(z, m).start()

        to_x(z, m).start()
        to_sib(z, m, 0).start()
    load_w.start()
    load_wo.start()

    @pl.when(z == size - 1)
    def _():
        move_noise.start()

    num[...] = jnp.zeros_like(num)
    den[...] = jnp.zeros_like(den)

    def forward(k):
        d, m = k // 2 + 1, k % 2

        @pl.when(z + d < size)
        def _():
            f = z + d
            to_right(f, m).wait_recv()

            @pl.when(has_left)
            def _():
                to_left(f, m).start()

            to_x(f, m).start()
            to_sib(f, m, 0).start()

        @pl.when(z - d >= 0)
        def _():
            f = z - d
            to_left(f, m).wait_recv()

            @pl.when(has_right)
            def _():
                to_right(f, m).start()

            to_x(f, m).start()
            to_sib(f, m, 0).start()

    def norm_unit(f, m):
        from_x(f, m).wait_recv()
        to_sib(f, m, 1).start()
        from_sib(f, m, 0).wait_recv()
        from_sib(f, m, 1).wait_recv()
        if m == 0:
            for q in range(4):
                cols = slice(q * wid, (q + 1) * wid)
                extra = lat[f, q, pl.ds(0, EXTRA), :].astype(F32)
                mods[0, :, cols] = jnp.broadcast_to(extra[0:1], (8, wid))
                mods[1, :, cols] = jnp.broadcast_to(1.0 + extra[1:2], (8, wid))

        def norm_rows(t, inner):
            r = pl.ds(pl.multiple_of(t * LN_ROWS + m * half, LN_ROWS), LN_ROWS)
            src = pl.ds(pl.multiple_of(t * LN_ROWS + m * half + EXTRA, LN_ROWS), LN_ROWS)
            parts = [lat[f, q, src, :].astype(F32) for q in range(4)]
            total = parts[0] + parts[1] + parts[2] + parts[3]
            mean = jnp.sum(total, axis=-1, keepdims=True) * (1.0 / full)
            parts = [part - mean for part in parts]
            squares = parts[0] * parts[0]
            for part in parts[1:]:
                squares = squares + part * part
            var = jnp.sum(squares, axis=-1, keepdims=True) * (1.0 / full)
            scale = lax.rsqrt(var + 1e-06)
            for q in range(4):
                cols = slice(q * wid, (q + 1) * wid)
                out = parts[q] * scale * mods[1, 0:1, cols] + mods[0, 0:1, cols]
                hid[r, cols] = out.astype(BF16)
            return inner

        lax.fori_loop(0, half // LN_ROWS, norm_rows, 0, unroll=4)

    def absorb_rows(rows, first):
        def one_pair(p, inner):
            cols = pl.ds(pl.multiple_of(p * 2 * HD, 2 * HD), 2 * HD)
            if first:

                @pl.when(p == 1)
                def _():
                    forward(2)

                q2 = jnp.dot(hid[...], w[0, :, cols], preferred_element_type=F32)
                halves = [
                    unit_rms(q2[:, i * HD : (i + 1) * HD]) / math.sqrt(HD) for i in range(2)
                ]
                qbuf[:, cols] = jnp.concatenate(halves, axis=1).astype(BF16)

            k2 = jnp.dot(hid[rows, :], w[1, :, cols], preferred_element_type=F32)
            keys = [unit_rms(k2[:, i * HD : (i + 1) * HD]).astype(BF16) for i in range(2)]
            values = jnp.dot(hid[rows, :], w[2, :, cols], preferred_element_type=F32).astype(BF16)
            for i in range(2):
                head = pl.ds(pl.multiple_of(p * 2 * HD + i * HD, HD), HD)
                scores = lax.dot_general(
                    qbuf[:, head], keys[i], (((1,), (1,)), ((), ())), preferred_element_type=F32
                )
                weights = jnp.exp(scores)
                den[:, head] += jnp.broadcast_to(
                    jnp.sum(weights, axis=1, keepdims=True), (tok, HD)
                )
                num[:, head] += jnp.dot(
                    weights.astype(BF16),
                    values[:, i * HD : (i + 1) * HD],
                    preferred_element_type=F32,
                )
            return inner

        lax.fori_loop(0, pairs, one_pair, 0)

    orders = frame_order(size)
    forward(0)
    norm_unit(z, 0)
    forward(1)
    norm_unit(z, 1)
    load_w.wait()
    absorb_rows(slice(0, tok), True)

    def step(s, carry):
        f = jnp.int32(0)
        for i in range(1, size):
            f = jnp.where(s == i, pick([o[i] for o in orders], z), f)
        norm_unit(f, 0)

        @pl.when(s == 1)
        def _():
            forward(3)

        absorb_rows(slice(0, half), False)
        norm_unit(f, 1)

        @pl.when(s == 1)
        def _():
            forward(4)

        @pl.when(s == 2)
        def _():
            forward(5)

        absorb_rows(slice(half, tok), False)

        return carry

    lax.fori_loop(1, size, step, 0)
    load_wo.wait()

    def chunk(r):
        return pl.ds(pl.multiple_of(r * rows, rows), rows)

    def token_rows(r):
        return pl.ds(pl.multiple_of(r * rows + EXTRA, LN_ROWS), rows)

    def sib_copy(r):
        return pltpu.make_async_remote_copy(
            sbuf.at[r], rbuf.at[r], tail_ss.at[r], tail_sr.at[r], {"ha": sib}, MESH
        )

    def x_copy(r):
        return pltpu.make_async_remote_copy(
            xbuf.at[r], xrecv.at[r], tail_xs.at[r], tail_xr.at[r], {"ha": xp}, MESH
        )

    def z_send(r):
        return pltpu.make_async_remote_copy(
            adv.at[r], nxt.at[r], tail_zs.at[r], tail_zr.at[r], {"pb": z - 1}, MESH
        )

    def z_recv(r):
        return pltpu.make_async_remote_copy(
            adv.at[r], nxt.at[r], tail_zs.at[r], tail_zr.at[r], {"pb": z + 1}, MESH
        )

    def adv_out(r):
        return pltpu.make_async_copy(adv.at[r], adv_hbm.at[0, chunk(r)], adv_sem.at[r])

    def nxt_out(r):
        return pltpu.make_async_copy(nxt.at[r], next_hbm.at[0, chunk(r)], nxt_sem.at[r])

    def project(att, quarter):
        cols = pl.ds(pl.multiple_of(quarter * wid, wid), wid)
        return jnp.dot(att, wo[:, cols], preferred_element_type=F32)

    def partials(t, carry):
        @pl.when(t < CHUNKS)
        def _():
            att = (num[chunk(t), :] / den[chunk(t), :]).astype(BF16)
            sbuf[t, 1] = project(att, far).astype(BF16)
            sbuf[t, 0] = project(att, sib).astype(BF16)
            sib_copy(t).start()
            xpart[t] = project(att, xp)
            own[t] = project(att, h)

        @pl.when(t >= 1)
        def _():
            r = t - 1
            sib_copy(r).wait_recv()
            xbuf[r] = (xpart[r] + rbuf[r, 1].astype(F32)).astype(BF16)
            x_copy(r).start()

        return carry

    lax.fori_loop(0, CHUNKS + 1, partials, 0)

    def finish(r, carry):
        x_copy(r).wait_recv()
        branch = own[r] + rbuf[r, 0].astype(F32) + xrecv[r].astype(F32)
        latent = lat[z, h, token_rows(r), :].astype(F32)
        adv[r] = (latent + gate[0:1] * branch).astype(BF16)

        @pl.when(has_left)
        def _():
            z_send(r).start()

        adv_out(r).start()
        return carry

    lax.fori_loop(0, CHUNKS, finish, 0)

    def drain_frames(f, carry):
        for m in range(2):
            to_x(f, m).wait_send()
            to_sib(f, m, 0).wait_send()
            to_sib(f, m, 1).wait_send()

            @pl.when(has_left & (f >= z))
            def _():
                to_left(f, m).wait_send()

            @pl.when(has_right & (f <= z))
            def _():
                to_right(f, m).wait_send()

        return carry

    lax.fori_loop(0, size, drain_frames, 0)

    def take_next(r, carry):
        @pl.when(has_right)
        def _():
            z_recv(r).wait_recv()
            nxt_out(r).start()

        return carry

    lax.fori_loop(0, CHUNKS, take_next, 0)

    def drain_tail(r, carry):
        sib_copy(r).wait_send()
        x_copy(r).wait_send()
        adv_out(r).wait()

        @pl.when(has_left)
        def _():
            z_send(r).wait_send()

        @pl.when(has_right)
        def _():
            nxt_out(r).wait()

        return carry

    lax.fori_loop(0, CHUNKS, drain_tail, 0)

    @pl.when(z == size - 1)
    def _():
        move_noise.wait()


def land_kernel(a_ref, b_ref, a_out, b_out):
    a_out[...] = a_ref[...]
    b_out[...] = b_ref[...]


def fused(size, latents, timesteps, mod_weight, qkv_weight, out_weight, noise_frame):
    _, tok, wid = latents.shape
    full = 4 * wid
    rows = tok // CHUNKS
    embedding = sinusoid(timesteps).astype(BF16)
    embedding = jnp.broadcast_to(embedding, (EXTRA, TDIM))
    anywhere = pl.BlockSpec(memory_space=pl.ANY)
    dma = pltpu.SemaphoreType.DMA
    flops = 2 * tok * full * wid * (1 + 2 * size) + 4 * tok * tok * size * wid + 2 * tok * wid * full
    outs = pl.pallas_call(
        functools.partial(block_kernel, size),
        out_shape=(
            jax.ShapeDtypeStruct(latents.shape, BF16),
            jax.ShapeDtypeStruct(latents.shape, BF16),
        ),
        in_specs=[pl.BlockSpec(memory_space=pltpu.VMEM)] + [anywhere] * 5,
        out_specs=(anywhere, anywhere),
        scratch_shapes=[
            pltpu.VMEM((size, 4, tok + EXTRA, wid), BF16),
            pltpu.VMEM((3, TDIM, wid), BF16),
            pltpu.VMEM((3, full, wid), BF16),
            pltpu.VMEM((wid, full), BF16),
            pltpu.VMEM((tok, full), BF16),
            pltpu.VMEM((2, 8, full), F32),
            pltpu.VMEM((8, wid), F32),
            pltpu.VMEM((tok, wid), BF16),
            pltpu.VMEM((tok, wid), F32),
            pltpu.VMEM((tok, wid), F32),
            pltpu.VMEM((CHUNKS, rows, wid), F32),
            pltpu.VMEM((CHUNKS, rows, wid), F32),
            pltpu.VMEM((CHUNKS, 2, rows, wid), BF16),
            pltpu.VMEM((CHUNKS, 2, rows, wid), BF16),
            pltpu.VMEM((CHUNKS, rows, wid), BF16),
            pltpu.VMEM((CHUNKS, rows, wid), BF16),
            pltpu.VMEM((CHUNKS, rows, wid), BF16),
            pltpu.VMEM((CHUNKS, rows, wid), BF16),
            dma((5,)),
            dma((2, size)),
            dma((2, size)),
            dma((2, size)),
            dma((2, 2, size)),
            dma((2, size)),
            dma((2, size)),
            dma((2, 2, size)),
            dma((CHUNKS,)),
            dma((CHUNKS,)),
            dma((CHUNKS,)),
            dma((CHUNKS,)),
            dma((CHUNKS,)),
            dma((CHUNKS,)),
            dma((CHUNKS,)),
            dma((CHUNKS,)),
        ],
        compiler_params=pltpu.CompilerParams(
            collective_id=0, has_side_effects=True, vmem_limit_bytes=58 * 1024 * 1024
        ),
        cost_estimate=pl.CostEstimate(
            flops=flops, bytes_accessed=22_000_000, transcendentals=tok * tok * size * wid // HD
        ),
    )(
        embedding,
        latents,
        mod_weight.transpose(1, 0, 2),
        qkv_weight.transpose(1, 0, 2),
        out_weight,
        noise_frame,
    )
    piece = pl.BlockSpec((1, tok, wid), lambda i: (0, 0, 0))
    return pl.pallas_call(
        land_kernel,
        grid=(1,),
        out_shape=(
            jax.ShapeDtypeStruct(latents.shape, BF16),
            jax.ShapeDtypeStruct(latents.shape, BF16),
        ),
        in_specs=[piece, piece],
        out_specs=(piece, piece),
    )(*outs)


def solution(mesh):
    placed = (
        P(("grp", "pb"), None, "ha"),
        P(("grp", "pb")),
        P(None, None, "ha"),
        P(None, None, "ha"),
        P("ha", None),
        P("grp", "ha"),
    )
    small = mesh.shape["ha"] == 4 and mesh.shape["pb"] <= 4
    return jax.shard_map(
        functools.partial(fused, mesh.shape["pb"]) if small else on_device,
        mesh=mesh,
        in_specs=placed,
        out_specs=(P(("grp", "pb"), None, "ha"), P(("grp", "pb"), None, "ha")),
        check_vma=False,
    )
```
